256 devices in a mesh: gx: 8 (over x, core), gy: 32 (over z, y).
Axes of the slice: x: 4, y: 4, z: 8, core: 2. Of those that a mesh axis runs over, the one named last changes fastest.
Arguments:
- state_field: float32 [256, 512, 16, 256], P('gx', 'gy'), may hold values from -80 to 80
- start_basis: float32 [256, 32], replicated, may hold values from -6 to 6
Outputs:
- core_tensor: float32 [256, 512, 512], P('gx', 'gy')
- z_factor: float32 [256, 32], replicated
- x_triangle: float32 [256, 256], replicated
The draws below stay inside these ranges and needn't reach their ends.
All inputs are finite; a program needn't handle non-finite values.
Results may differ from the reference program's by a relative error of at most 0.0003.
Values sent between devices are 32-bit elements; how exact they have to be, the bound alone decides.
A program may use at most 64 MiB of HBM per device.

```python
import math
import jax
import jax.numpy as jnp
from jax import lax

NZ = 256
NS = 16
RZ = 32
ITERS = 3
NX = 256
NY = 512


def draw_state_field(key, part):
    noise_key = jax.random.fold_in(key, 11)
    zscale_key = jax.random.fold_in(key, 12)
    sscale_key = jax.random.fold_in(key, 13)
    noise = jax.random.truncated_normal(noise_key, -4.0, 4.0, (NX, NY, NS, NZ), jnp.float32)
    z_scale = jnp.exp(jax.random.uniform(zscale_key, (NZ,), jnp.float32, math.log(0.3), math.log(3.0)))
    s_scale = jnp.exp(jax.random.uniform(sscale_key, (NS,), jnp.float32, math.log(0.5), math.log(2.0)))
    x_ramp = jnp.exp(math.log(3.0) * jnp.arange(NX, dtype=jnp.float32) / NX)
    y_ramp = jnp.exp(math.log(3.0) * jnp.arange(NY, dtype=jnp.float32) / NY)
    amplitude = 0.3 * x_ramp[:, None] * y_ramp[None, :]
    field_values = noise * amplitude[:, :, None, None] * s_scale[None, None, :, None] * z_scale[None, None, None, :]
    return field_values


def scatter_about(key, extent, spread, limit, held_as=jnp.bfloat16):
    values = spread * jax.random.normal(key, extent, jnp.float32)
    return jnp.clip(values, min=-limit, max=limit).astype(held_as)


def setup_inputs(seed: int = 0) -> dict:
    keys = jax.random.split(jax.random.key(seed), 3)
    return {
        "state_field": draw_state_field(jax.random.fold_in(keys[2], 71), 0),
        "start_basis": scatter_about(keys[1], (NZ, RZ), 1.0, 6.0, jnp.float32),
    }


precise = lax.Precision.HIGHEST

def orthonormal(image):
    for repeat in range(2):
        inner_gram = jnp.dot(image.T.astype(jnp.float32), image.astype(jnp.float32), precision=precise, preferred_element_type=jnp.float32)
        lower_factor = jnp.linalg.cholesky(inner_gram)
        image = lax.linalg.triangular_solve(lower_factor, image, left_side=False, lower=True, transpose_a=True)
    return image

def reference(state_field, start_basis):
    unfolded = state_field.reshape(-1, NZ)
    gram_z = lax.dot_general(unfolded.astype(jnp.float32), unfolded.astype(jnp.float32), (((0,), (0,)), ((), ())), precision=precise, preferred_element_type=jnp.float32)
    z_basis = start_basis
    for iteration in range(ITERS):
        z_basis = orthonormal(jnp.dot(gram_z.astype(jnp.float32), z_basis.astype(jnp.float32), precision=precise, preferred_element_type=jnp.float32))
    core_rows = jnp.dot(unfolded.astype(jnp.float32), z_basis.astype(jnp.float32), precision=precise, preferred_element_type=jnp.float32)
    core_tensor = core_rows.reshape(NX, NY, NS * RZ)
    x_rows = core_tensor.reshape(NX, -1)
    gram_x = jnp.dot(x_rows.astype(jnp.float32), x_rows.T.astype(jnp.float32), precision=precise, preferred_element_type=jnp.float32)
    x_triangle = jnp.linalg.cholesky(gram_x).T / jnp.sqrt(jnp.float32(NY * NS * RZ))
    return (core_tensor, z_basis, x_triangle)
```

```python
import functools
import math

import jax
import jax.numpy as jnp
from jax import lax
from jax.experimental import pallas as pl
from jax.experimental.pallas import tpu as pltpu
from jax.sharding import PartitionSpec as P

ITERS = 3
LANES = 128
SUBLANES = 8
MESH = pl.DeviceIdType.MESH
F32 = jnp.float32
BF16 = jnp.bfloat16
VMEM_LIMIT = 48 * 2**20

NX_CHIPS = 4
NY_CHIPS = 4
NZ_CHIPS = 8
CORES = 2
PLANE = NX_CHIPS * NY_CHIPS


def split3(value):
    high = value.astype(BF16)
    rest = value - high.astype(F32)
    middle = rest.astype(BF16)
    low = (rest - middle.astype(F32)).astype(BF16)
    return high, middle, low


def contract(left, right, left_dim, right_dim, precision=None):
    return lax.dot_general(
        left,
        right,
        (((left_dim,), (right_dim,)), ((), ())),
        precision=precision,
        preferred_element_type=F32,
    )


def lane_spread(block, lane):
    picks = jnp.full((SUBLANES, LANES), lane, jnp.int32)
    return jnp.take_along_axis(block, picks, axis=1, mode="promise_in_bounds")


def row_spread(block, row):
    return jnp.broadcast_to(block[row : row + 1, :], block.shape)


def eliminate(rows, tile, lane0):
    groups = len(rows)
    tiles = len(rows[0])
    rows = [list(group) for group in rows]
    sublane = lax.broadcasted_iota(jnp.int32, (SUBLANES, LANES), 0)
    scales = []
    for p in range(groups):
        columns = [
            [
                lane_spread(rows[q][tile], lane0 + SUBLANES * p + j) if q >= p else None
                for q in range(groups)
            ]
            for j in range(SUBLANES)
        ]
        scale = jnp.zeros((SUBLANES, LANES), F32)
        for j in range(SUBLANES):
            pivot = row_spread(columns[j][p], j)
            scale = jnp.where(sublane == j, lax.rsqrt(pivot), scale)
            inverse = 1.0 / pivot
            below = [q for q in range(p, groups) if not (q == p and j == SUBLANES - 1)]
            factor = {}
            for q in below:
                factor[q] = columns[j][q] * inverse
                if q == p:
                    factor[q] = jnp.where(sublane > j, factor[q], 0.0)
            for later in range(j + 1, SUBLANES):
                entry = row_spread(columns[later][p], j)
                for q in below:
                    columns[later][q] = columns[later][q] - factor[q] * entry
            for t in range(tiles):
                pivot_row = row_spread(rows[p][t], j)
                for q in below:
                    rows[q][t] = rows[q][t] - factor[q] * pivot_row
        scales.append(scale)
    return [[rows[q][t] * scales[q] for t in range(tiles)] for q in range(groups)]


def to_blocks(matrix):
    rows, columns = matrix.shape
    return [
        [
            matrix[r : r + SUBLANES, c : c + LANES]
            for c in range(0, columns, LANES)
        ]
        for r in range(0, rows, SUBLANES)
    ]


def from_blocks(blocks):
    return jnp.concatenate([jnp.concatenate(group, axis=1) for group in blocks], axis=0)


HIGHEST = lax.Precision.HIGHEST


def orthonormal(image_t):
    rank = image_t.shape[0]
    for repeat in range(2):
        inner_gram = contract(image_t, image_t, 1, 1, HIGHEST)
        padded = jnp.concatenate(
            [inner_gram, jnp.zeros((rank, LANES - rank), F32)], axis=1
        )
        blocks = [
            [c[0]] + w for c, w in zip(to_blocks(padded), to_blocks(image_t))
        ]
        blocks = eliminate(blocks, 0, 0)
        image_t = from_blocks([group[1:] for group in blocks])
    return image_t


def position():
    gx = lax.axis_index("gx")
    gy = lax.axis_index("gy")
    return gx // CORES, gx % CORES, gy % NY_CHIPS, gy // NY_CHIPS


def device(x, core, y, z):
    return (x * CORES + core, z * NY_CHIPS + y)


def far_first(steps):
    def hops(step):
        return sum(min(d, n - d) for d, n in zip(step, (NX_CHIPS, NY_CHIPS)))

    return sorted(steps, key=hops, reverse=True)


PLANE_STEPS = far_first(
    [(i, j) for i in range(NX_CHIPS) for j in range(NY_CHIPS) if i or j]
)
Z_STEPS = sorted(range(1, NZ_CHIPS), key=lambda d: -min(d, NZ_CHIPS - d))


def remote(source, target, send_sem, recv_sem, where):
    return pltpu.make_async_remote_copy(
        src_ref=source,
        dst_ref=target,
        send_sem=send_sem,
        recv_sem=recv_sem,
        device_id=where,
        device_id_type=MESH,
    )


def all_reduce(partial, full, from_core, mine, plane_in, z_out, z_in, send, recv):
    x, core, y, z = position()
    half = partial.shape[0] // CORES
    strip = half // PLANE
    place = x * NY_CHIPS + y
    own_half = pl.multiple_of(core * half, half)
    other_half = pl.multiple_of((1 - core) * half, half)
    other_core = device(x, 1 - core, y, z)

    swap = remote(
        partial.at[pl.ds(other_half, half)], from_core, send.at[0], recv.at[0], other_core
    )
    swap.start()
    swap.wait()
    summed = partial[pl.ds(own_half, half), :] + from_core[...]
    mine[...] = summed.reshape(mine.shape)

    for i, j in PLANE_STEPS:
        to_x, to_y = (x + i) % NX_CHIPS, (y + j) % NY_CHIPS
        remote(
            mine.at[to_x * NY_CHIPS + to_y],
            plane_in.at[place],
            send.at[1],
            recv.at[1],
            device(to_x, core, to_y, z),
        ).start()
    plane_in[place] = mine[place]
    others = pl.ds(0, PLANE - 1)
    landed = remote(mine.at[others], plane_in.at[others], send.at[1], recv.at[1], other_core)
    landed.wait()
    total = plane_in[0]
    for k in range(1, PLANE):
        total = total + plane_in[k]

    z_out[...] = total
    z_in[z] = total
    for d in Z_STEPS:
        to_z = (z + d) % NZ_CHIPS
        remote(
            z_out, z_in.at[z], send.at[2], recv.at[2], device(x, core, y, to_z)
        ).start()
    others = pl.ds(0, NZ_CHIPS - 1)
    landed = remote(z_in.at[others], z_in.at[others], send.at[2], recv.at[2], other_core)
    landed.wait()
    total = z_in[0]
    for k in range(1, NZ_CHIPS):
        total = total + z_in[k]

    own_strip = pl.ds(pl.multiple_of(own_half + place * strip, strip), strip)
    full[own_strip, :] = total
    for i, j in PLANE_STEPS:
        to_x, to_y = (x + i) % NX_CHIPS, (y + j) % NY_CHIPS
        remote(
            full.at[own_strip],
            full.at[own_strip],
            send.at[3],
            recv.at[3],
            device(to_x, core, to_y, z),
        ).start()
    others = pl.ds(0, (PLANE - 1) * strip)
    landed = remote(full.at[others], full.at[others], send.at[3], recv.at[3], other_core)
    landed.wait()

    rows = pl.ds(own_half, half)
    swap = remote(full.at[rows], full.at[rows], send.at[4], recv.at[4], other_core)
    swap.start()
    swap.wait()


def main_kernel(
    field,
    basis,
    core_out,
    zt_out,
    gram_x_out,
    staged,
    acc_same,
    acc_cross,
    partial,
    gram_z,
    gram_x,
    weights,
    core_parts,
    regrouped,
    *scratch,
):
    reduce_z, reduce_x = scratch[0:5], scratch[5:10]
    send_z, recv_z, send_x, recv_x, load_sem, core_sem, cell_send, cell_recv = scratch[10:]
    x, core, y, z = position()
    gx = x * CORES + core
    species = staged.shape[0]
    x_cells, y_cells, nz = staged.shape[1:]
    cells = x_cells * y_cells
    rank = basis.shape[1]
    groups = species * rank // LANES
    per_group = species // groups

    for s in range(species):
        pltpu.make_async_copy(field.at[:, :, s, :], staged.at[s], load_sem.at[s]).start()

    barrier = pltpu.get_barrier_semaphore()
    partners = [device(x, 1 - core, y, z)]
    for i, j in PLANE_STEPS:
        partners.append(device((x + i) % NX_CHIPS, core, (y + j) % NY_CHIPS, z))
    for d in Z_STEPS:
        partners.append(device(x, core, y, (z + d) % NZ_CHIPS))
    for i in range(1, NX_CHIPS):
        partners.append(device((x + i) % NX_CHIPS, 1 - core, y, z))
    for partner in partners:
        pl.semaphore_signal(barrier, inc=1, device_id=partner, device_id_type=MESH)

    acc_same[...] = jnp.zeros_like(acc_same)
    acc_cross[...] = jnp.zeros_like(acc_cross)

    def gram_step(s, carry):
        pltpu.make_async_copy(field.at[:, :, 0, :], staged.at[0], load_sem.at[s]).wait()
        high, middle, low = split3(staged[s].reshape(cells, nz))
        acc_same[...] += contract(high, high, 0, 0) + contract(middle, middle, 0, 0)
        acc_cross[...] += contract(high, middle, 0, 0) + contract(high, low, 0, 0)
        return carry

    lax.fori_loop(0, species, gram_step, 0)
    cross = acc_cross[...]
    partial[...] = acc_same[...] + (cross + cross.T)

    pl.semaphore_wait(barrier, len(partners))
    all_reduce(partial, gram_z, *reduce_z, send_z, recv_z)

    basis_t = basis[...].T
    for iteration in range(ITERS):
        basis_t = orthonormal(contract(basis_t, gram_z[...], 1, 0, HIGHEST))
    zt_out[...] = basis_t

    z_high, z_middle, _ = split3(basis_t)
    weights[...] = jnp.zeros_like(weights)
    for k in range(per_group):
        weights[k, k * rank : (k + 1) * rank, :] = z_high
        weights[k, LANES + k * rank : LANES + (k + 1) * rank, :] = z_middle

    half_y = y_cells // CORES
    for step in (2, 1, 3, 0):
        g = (x + step) % NX_CHIPS
        chunk = 4

        def core_step(i, carry):
            rows = pl.ds(i * chunk, chunk)
            total = jnp.zeros((chunk * y_cells, 2 * LANES), F32)
            for k in range(per_group):
                part = staged[g * per_group + k, rows].reshape(chunk * y_cells, nz)
                high = part.astype(BF16)
                middle = (part - high.astype(F32)).astype(BF16)
                total += contract(high, weights[k], 1, 1) + contract(middle, weights[k], 1, 1)
            core_parts[g, rows] = (total[:, :LANES] + total[:, LANES:]).reshape(
                chunk, y_cells, LANES
            )
            return carry

        lax.fori_loop(0, x_cells // chunk, core_step, 0)
        pltpu.make_async_copy(
            core_parts.at[g],
            core_out.at[:, :, pl.ds(pl.multiple_of(g * LANES, LANES), LANES)],
            core_sem.at[step],
        ).start()
        if step:
            for h in range(CORES):
                remote(
                    core_parts.at[g, :, pl.ds(h * half_y, half_y), :],
                    regrouped.at[gx],
                    cell_send,
                    cell_recv,
                    device(g, h, y, z),
                ).start()
        else:
            there = pl.multiple_of((1 - core) * half_y, half_y)
            remote(
                core_parts.at[g, :, pl.ds(there, half_y), :],
                regrouped.at[gx],
                cell_send,
                cell_recv,
                device(x, 1 - core, y, z),
            ).start()
            here = pl.multiple_of(core * half_y, half_y)
            regrouped[gx] = core_parts[g, :, pl.ds(here, half_y), :]

    others = pl.ds(0, CORES * NX_CHIPS - 1)
    landed = remote(
        regrouped.at[others], regrouped.at[others], cell_send, cell_recv, partners[0]
    )
    landed.wait()

    total_rows = regrouped.shape[0] * x_cells
    table = regrouped.reshape(total_rows * half_y, LANES)
    same = jnp.zeros((total_rows, total_rows), F32)
    cross = jnp.zeros((total_rows, total_rows), F32)
    for pair in range(half_y // 2):
        both = jnp.concatenate(
            [table[pl.ds(2 * pair + i, total_rows, stride=half_y), :] for i in range(2)],
            axis=1,
        )
        high, middle, low = split3(both)
        same += contract(high, high, 1, 1) + contract(middle, middle, 1, 1)
        cross += contract(high, middle, 1, 1) + contract(high, low, 1, 1)
    partial[...] = same + (cross + cross.T)
    all_reduce(partial, gram_x, *reduce_x, send_x, recv_x)
    gram_x_out[...] = gram_x[...]
    for g in range(groups):
        pltpu.make_async_copy(
            core_parts.at[0], core_out.at[:, :, pl.ds(0, LANES)], core_sem.at[g]
        ).wait()


def finish_kernel(column_count, core_in, zt, gram_x, core_out, z_out, tri_out, upper, sem):
    copy = pltpu.make_async_copy(core_in, core_out, sem)
    copy.start()
    z_out[...] = zt[...].T
    size = gram_x.shape[0]
    block = 32
    scale = 1.0 / math.sqrt(column_count)
    for r in range(0, size, block):
        first = r // LANES * LANES
        here = gram_x[r : r + block, first:]
        if r:
            here = here - contract(
                upper[0:r, r : r + block], upper[0:r, first:], 0, 0, HIGHEST
            )
        done = from_blocks(eliminate(to_blocks(here), 0, r - first))
        row = lax.broadcasted_iota(jnp.int32, done.shape, 0) + r
        column = lax.broadcasted_iota(jnp.int32, done.shape, 1) + first
        done = jnp.where(column >= row, done, 0.0)
        upper[r : r + block, first:] = done
        tri_out[r : r + block, first:] = done * scale
        if first:
            tri_out[r : r + block, :first] = jnp.zeros((block, first), F32)
    copy.wait()


def local(state_field, start_basis):
    x_cells, y_cells, species, nz = state_field.shape
    rank = start_basis.shape[1]
    columns = species * rank
    x_total = x_cells * lax.axis_size("gx")
    groups = columns // LANES
    half_y = y_cells // CORES
    vmem = pl.BlockSpec(memory_space=pltpu.VMEM)
    anywhere = pl.BlockSpec(memory_space=pl.ANY)

    def reduce_buffers(size):
        half = size // CORES
        strip = half // PLANE
        return [
            pltpu.VMEM((half, size), F32),
            pltpu.VMEM((PLANE, strip, size), F32),
            pltpu.VMEM((PLANE, strip, size), F32),
            pltpu.VMEM((strip, size), F32),
            pltpu.VMEM((NZ_CHIPS, strip, size), F32),
        ]

    dma = pltpu.SemaphoreType.DMA
    core_tensor, zt, gram_x = pl.pallas_call(
        main_kernel,
        out_shape=(
            jax.ShapeDtypeStruct((x_cells, y_cells, columns), F32),
            jax.ShapeDtypeStruct((rank, nz), F32),
            jax.ShapeDtypeStruct((x_total, x_total), F32),
        ),
        in_specs=[anywhere, vmem],
        out_specs=(anywhere, vmem, vmem),
        scratch_shapes=[
            pltpu.VMEM((species, x_cells, y_cells, nz), F32),
            pltpu.VMEM((nz, nz), F32),
            pltpu.VMEM((nz, nz), F32),
            pltpu.VMEM((nz, nz), F32),
            pltpu.VMEM((nz, nz), F32),
            pltpu.VMEM((x_total, x_total), F32),
            pltpu.VMEM((species // groups, 2 * LANES, nz), BF16),
            pltpu.VMEM((groups, x_cells, y_cells, LANES), F32),
            pltpu.VMEM((CORES * NX_CHIPS, x_cells, half_y, LANES), F32),
            *reduce_buffers(nz),
            *reduce_buffers(x_total),
            dma((5,)),
            dma((5,)),
            dma((5,)),
            dma((5,)),
            dma((species,)),
            dma((groups,)),
            dma,
            dma,
        ],
        compiler_params=pltpu.CompilerParams(
            collective_id=0, has_side_effects=True, vmem_limit_bytes=VMEM_LIMIT
        ),
        name="basis_core_gram",
    )(state_field, start_basis)

    column_count = y_cells * lax.axis_size("gy") * columns
    return pl.pallas_call(
        functools.partial(finish_kernel, column_count),
        out_shape=(
            jax.ShapeDtypeStruct((x_cells, y_cells, columns), F32),
            jax.ShapeDtypeStruct((nz, rank), F32),
            jax.ShapeDtypeStruct((x_total, x_total), F32),
        ),
        in_specs=[anywhere, vmem, vmem],
        out_specs=(anywhere, vmem, vmem),
        scratch_shapes=[pltpu.VMEM((x_total, x_total), F32), dma],
        compiler_params=pltpu.CompilerParams(vmem_limit_bytes=VMEM_LIMIT),
        name="x_factor",
    )(core_tensor, zt, gram_x)


def solution(mesh):
    return jax.shard_map(
        local,
        mesh=mesh,
        in_specs=(P("gx", "gy", None, None), P()),
        out_specs=(P("gx", "gy", None), P(), P()),
        check_vma=False,
    )
```

```python
import functools
import math

import jax
import jax.numpy as jnp
from jax import lax
from jax.experimental import pallas as pl
from jax.experimental.pallas import tpu as pltpu
from jax.sharding import PartitionSpec as P

ITERS = 3
LANES = 128
SUBLANES = 8
MESH = pl.DeviceIdType.MESH
F32 = jnp.float32
BF16 = jnp.bfloat16
VMEM_LIMIT = 48 * 2**20

NX_CHIPS = 4
NY_CHIPS = 4
NZ_CHIPS = 8
CORES = 2
PLANE = NX_CHIPS * NY_CHIPS


def split3(value):
    high = value.astype(BF16)
    rest = value - high.astype(F32)
    middle = rest.astype(BF16)
    low = (rest - middle.astype(F32)).astype(BF16)
    return high, middle, low


def split2(value):
    high = value.astype(BF16)
    return high, (value - high.astype(F32)).astype(BF16)


def contract(left, right, left_dim, right_dim, precision=None):
    return lax.dot_general(
        left,
        right,
        (((left_dim,), (right_dim,)), ((), ())),
        precision=precision,
        preferred_element_type=F32,
    )


def lane_spread(block, lane):
    picks = jnp.full((SUBLANES, LANES), lane, jnp.int32)
    return jnp.take_along_axis(block, picks, axis=1, mode="promise_in_bounds")


def row_spread(block, row):
    return jnp.broadcast_to(block[row : row + 1, :], block.shape)


def eliminate(rows, tile, lane0):
    groups = len(rows)
    tiles = len(rows[0])
    rows = [list(group) for group in rows]
    sublane = lax.broadcasted_iota(jnp.int32, (SUBLANES, LANES), 0)
    steps = range(SUBLANES)
    for p in range(groups):
        below = range(p + 1, groups)
        columns = [
            {q: lane_spread(rows[q][tile], lane0 + SUBLANES * p + j) for q in range(p, groups)}
            for j in steps
        ]
        corner = {(j, l): row_spread(columns[l][p], j) for j in steps for l in range(j, SUBLANES)}
        lines = [[row_spread(rows[p][t], j) for j in steps] for t in range(tiles)]
        done = list(rows[p])
        for j in steps:
            inverse = 1.0 / corner[j, j]
            scale = lax.rsqrt(corner[j, j])
            for l in range(j + 1, SUBLANES):
                share = corner[j, l] * inverse
                for n in range(l, SUBLANES):
                    corner[l, n] = corner[l, n] - share * corner[j, n]
                for t in range(tiles):
                    lines[t][l] = lines[t][l] - share * lines[t][j]
            for q in below:
                factor = columns[j][q] * inverse
                for later in range(j + 1, SUBLANES):
                    columns[later][q] = columns[later][q] - factor * corner[j, later]
                for t in range(tiles):
                    rows[q][t] = rows[q][t] - factor * lines[t][j]
            for t in range(tiles):
                done[t] = jnp.where(sublane == j, lines[t][j] * scale, done[t])
        rows[p] = done
    return rows


def to_blocks(matrix):
    rows, columns = matrix.shape
    return [
        [
            matrix[r : r + SUBLANES, c : c + LANES]
            for c in range(0, columns, LANES)
        ]
        for r in range(0, rows, SUBLANES)
    ]


def from_blocks(blocks):
    return jnp.concatenate([jnp.concatenate(group, axis=1) for group in blocks], axis=0)


HIGHEST = lax.Precision.HIGHEST


def orthonormal(image_t):
    rank = image_t.shape[0]
    def one(r, image_t):
        inner_gram = contract(image_t, image_t, 1, 1, HIGHEST)
        padded = jnp.concatenate(
            [inner_gram, jnp.zeros((rank, LANES - rank), F32)], axis=1
        )
        blocks = [
            [c[0]] + w for c, w in zip(to_blocks(padded), to_blocks(image_t))
        ]
        blocks = eliminate(blocks, 0, 0)
        return from_blocks([group[1:] for group in blocks])
    return lax.fori_loop(0, 2, one, image_t)


def position():
    gx = lax.axis_index("gx")
    gy = lax.axis_index("gy")
    return gx // CORES, gx % CORES, gy % NY_CHIPS, gy // NY_CHIPS


def device(x, core, y, z):
    return (x * CORES + core, z * NY_CHIPS + y)


def far_first(steps):
    def hops(step):
        return sum(min(d, n - d) for d, n in zip(step, (NX_CHIPS, NY_CHIPS)))

    return sorted(steps, key=hops, reverse=True)


PLANE_STEPS = far_first(
    [(i, j) for i in range(NX_CHIPS) for j in range(NY_CHIPS) if i or j]
)
Z_STEPS = sorted(range(1, NZ_CHIPS), key=lambda d: -min(d, NZ_CHIPS - d))


def remote(source, target, send_sem, recv_sem, where):
    return pltpu.make_async_remote_copy(
        src_ref=source,
        dst_ref=target,
        send_sem=send_sem,
        recv_sem=recv_sem,
        device_id=where,
        device_id_type=MESH,
    )


def all_reduce(partial, full, from_core, mine, plane_in, z_out, z_in, send, recv):
    x, core, y, z = position()
    half = partial.shape[0] // CORES
    strip = half // PLANE
    place = x * NY_CHIPS + y
    own_half = pl.multiple_of(core * half, half)
    other_half = pl.multiple_of((1 - core) * half, half)
    other_core = device(x, 1 - core, y, z)

    swap = remote(
        partial.at[pl.ds(other_half, half)], from_core, send.at[0], recv.at[0], other_core
    )
    swap.start()
    swap.wait()
    summed = partial[pl.ds(own_half, half), :] + from_core[...]
    mine[...] = summed.reshape(mine.shape)

    for i, j in PLANE_STEPS:
        to_x, to_y = (x + i) % NX_CHIPS, (y + j) % NY_CHIPS
        remote(
            mine.at[to_x * NY_CHIPS + to_y],
            plane_in.at[place],
            send.at[1],
            recv.at[1],
            device(to_x, core, to_y, z),
        ).start()
    plane_in[place] = mine[place]
    others = pl.ds(0, PLANE - 1)
    landed = remote(mine.at[others], plane_in.at[others], send.at[1], recv.at[1], other_core)
    landed.wait()
    total = plane_in[0]
    for k in range(1, PLANE):
        total = total + plane_in[k]

    z_out[...] = total
    z_in[z] = total
    for d in Z_STEPS:
        to_z = (z + d) % NZ_CHIPS
        remote(
            z_out, z_in.at[z], send.at[2], recv.at[2], device(x, core, y, to_z)
        ).start()
    others = pl.ds(0, NZ_CHIPS - 1)
    landed = remote(z_in.at[others], z_in.at[others], send.at[2], recv.at[2], other_core)
    landed.wait()
    total = z_in[0]
    for k in range(1, NZ_CHIPS):
        total = total + z_in[k]

    own_strip = pl.ds(pl.multiple_of(own_half + place * strip, strip), strip)
    full[own_strip, :] = total
    for i, j in PLANE_STEPS:
        to_x, to_y = (x + i) % NX_CHIPS, (y + j) % NY_CHIPS
        remote(
            full.at[own_strip],
            full.at[own_strip],
            send.at[3],
            recv.at[3],
            device(to_x, core, to_y, z),
        ).start()
    others = pl.ds(0, (PLANE - 1) * strip)
    landed = remote(full.at[others], full.at[others], send.at[3], recv.at[3], other_core)
    landed.wait()

    rows = pl.ds(own_half, half)
    swap = remote(full.at[rows], full.at[rows], send.at[4], recv.at[4], other_core)
    swap.start()
    swap.wait()


def main_kernel(
    field,
    basis,
    core_out,
    zt_out,
    gram_x_out,
    staged,
    acc_same,
    acc_cross,
    partial,
    gram_z,
    gram_x,
    weights,
    core_parts,
    regrouped,
    *scratch,
):
    reduce_z, reduce_x = scratch[0:5], scratch[5:10]
    send_z, recv_z, send_x, recv_x, load_sem, core_sem, cell_send, cell_recv = scratch[10:]
    x, core, y, z = position()
    gx = x * CORES + core
    species = staged.shape[0]
    x_cells, y_cells, nz = staged.shape[1:]
    cells = x_cells * y_cells
    rank = basis.shape[0]
    groups = species * rank // LANES
    per_group = species // groups

    for s in range(species):
        pltpu.make_async_copy(field.at[:, :, s, :], staged.at[s], load_sem.at[s]).start()

    barrier = pltpu.get_barrier_semaphore()
    partners = [device(x, 1 - core, y, z)]
    for i, j in PLANE_STEPS:
        partners.append(device((x + i) % NX_CHIPS, core, (y + j) % NY_CHIPS, z))
    for d in Z_STEPS:
        partners.append(device(x, core, y, (z + d) % NZ_CHIPS))
    for i in range(1, NX_CHIPS):
        partners.append(device((x + i) % NX_CHIPS, 1 - core, y, z))
    for partner in partners:
        pl.semaphore_signal(barrier, inc=1, device_id=partner, device_id_type=MESH)

    acc_same[...] = jnp.zeros_like(acc_same)
    acc_cross[...] = jnp.zeros_like(acc_cross)

    batch = 4

    def gram_step(i, carry):
        for s in range(batch):
            pltpu.make_async_copy(
                field.at[:, :, 0, :], staged.at[0], load_sem.at[i * batch + s]
            ).wait()
        slab = staged[pl.ds(i * batch, batch)].reshape(batch * cells, nz)
        high, middle = split2(slab)
        acc_same[...] += contract(high, high, 0, 0) + contract(middle, middle, 0, 0)
        acc_cross[...] += contract(high, middle, 0, 0)
        return carry

    lax.fori_loop(0, species // batch, gram_step, 0)
    cross = acc_cross[...]
    partial[...] = acc_same[...] + (cross + cross.T)

    pl.semaphore_wait(barrier, len(partners))
    all_reduce(partial, gram_z, *reduce_z, send_z, recv_z)

    basis_t = basis[...]
    basis_t = lax.fori_loop(0, ITERS, lambda i, w: orthonormal(contract(w, gram_z[...], 1, 0, HIGHEST)), basis_t)
    zt_out[...] = basis_t

    z_high, z_middle = split2(basis_t)
    weights[...] = jnp.zeros_like(weights)
    for k in range(per_group):
        weights[k, k * rank : (k + 1) * rank, :] = z_high
        weights[k, LANES + k * rank : LANES + (k + 1) * rank, :] = z_middle

    half_y = y_cells // CORES
    for step in (2, 1, 3, 0):
        g = (x + step) % NX_CHIPS
        total = jnp.zeros((cells, 2 * LANES), F32)
        for k in range(per_group):
            part = staged[g * per_group + k].reshape(cells, nz)
            high, middle = split2(part)
            total += contract(high, weights[k], 1, 1) + contract(middle, weights[k], 1, 1)
        core_parts[g] = (total[:, :LANES] + total[:, LANES:]).reshape(
            x_cells, y_cells, LANES
        )
        pltpu.make_async_copy(
            core_parts.at[g],
            core_out.at[:, :, pl.ds(pl.multiple_of(g * LANES, LANES), LANES)],
            core_sem.at[step],
        ).start()
        if step:
            for h in range(CORES):
                remote(
                    core_parts.at[g, :, pl.ds(h * half_y, half_y), :],
                    regrouped.at[gx],
                    cell_send,
                    cell_recv,
                    device(g, h, y, z),
                ).start()
        else:
            there = pl.multiple_of((1 - core) * half_y, half_y)
            remote(
                core_parts.at[g, :, pl.ds(there, half_y), :],
                regrouped.at[gx],
                cell_send,
                cell_recv,
                device(x, 1 - core, y, z),
            ).start()
            here = pl.multiple_of(core * half_y, half_y)
            regrouped[gx] = core_parts[g, :, pl.ds(here, half_y), :]

    others = pl.ds(0, CORES * NX_CHIPS - 1)
    landed = remote(
        regrouped.at[others], regrouped.at[others], cell_send, cell_recv, partners[0]
    )
    landed.wait()

    total_rows = regrouped.shape[0] * x_cells
    table = regrouped.reshape(total_rows * half_y, LANES)
    same = jnp.zeros((total_rows, total_rows), F32)
    cross = jnp.zeros((total_rows, total_rows), F32)
    for pair in range(half_y // 2):
        both = jnp.concatenate(
            [table[pl.ds(2 * pair + i, total_rows, stride=half_y), :] for i in range(2)],
            axis=1,
        )
        high, middle, low = split3(both)
        same += contract(high, high, 1, 1) + contract(middle, middle, 1, 1)
        cross += contract(high, middle, 1, 1) + contract(high, low, 1, 1)
    partial[...] = same + (cross + cross.T)
    all_reduce(partial, gram_x, *reduce_x, send_x, recv_x)
    gram_x_out[...] = gram_x[...]
    for g in range(groups):
        pltpu.make_async_copy(
            core_parts.at[0], core_out.at[:, :, pl.ds(0, LANES)], core_sem.at[g]
        ).wait()


def finish_kernel(column_count, core_in, zt, gram_x, core_out, z_out, tri_out, upper, sem):
    copy = pltpu.make_async_copy(core_in, core_out, sem)
    copy.start()
    z_out[...] = zt[...]
    size = gram_x.shape[0]
    block = 64
    scale = 1.0 / math.sqrt(column_count)
    for r in range(0, size, block):
        first = r // LANES * LANES
        here = gram_x[r : r + block, first:]
        if r:
            here = here - contract(
                upper[0:r, r : r + block], upper[0:r, first:], 0, 0, HIGHEST
            )
        done = from_blocks(eliminate(to_blocks(here), 0, r - first))
        row = lax.broadcasted_iota(jnp.int32, done.shape, 0) + r
        column = lax.broadcasted_iota(jnp.int32, done.shape, 1) + first
        done = jnp.where(column >= row, done, 0.0)
        upper[r : r + block, first:] = done
        tri_out[r : r + block, first:] = done * scale
        if first:
            tri_out[r : r + block, :first] = jnp.zeros((block, first), F32)
    copy.wait()


def local(state_field, start_basis):
    x_cells, y_cells, species, nz = state_field.shape
    rank = start_basis.shape[1]
    columns = species * rank
    x_total = x_cells * lax.axis_size("gx")
    groups = columns // LANES
    half_y = y_cells // CORES
    vmem = pl.BlockSpec(memory_space=pltpu.VMEM)
    anywhere = pl.BlockSpec(memory_space=pl.ANY)

    def reduce_buffers(size):
        half = size // CORES
        strip = half // PLANE
        return [
            pltpu.VMEM((half, size), F32),
            pltpu.VMEM((PLANE, strip, size), F32),
            pltpu.VMEM((PLANE, strip, size), F32),
            pltpu.VMEM((strip, size), F32),
            pltpu.VMEM((NZ_CHIPS, strip, size), F32),
        ]

    dma = pltpu.SemaphoreType.DMA
    core_tensor, zt, gram_x = pl.pallas_call(
        main_kernel,
        out_shape=(
            jax.ShapeDtypeStruct((x_cells, y_cells, columns), F32),
            jax.ShapeDtypeStruct((rank, nz), F32),
            jax.ShapeDtypeStruct((x_total, x_total), F32),
        ),
        in_specs=[anywhere, vmem],
        out_specs=(anywhere, vmem, vmem),
        scratch_shapes=[
            pltpu.VMEM((species, x_cells, y_cells, nz), F32),
            pltpu.VMEM((nz, nz), F32),
            pltpu.VMEM((nz, nz), F32),
            pltpu.VMEM((nz, nz), F32),
            pltpu.VMEM((nz, nz), F32),
            pltpu.VMEM((x_total, x_total), F32),
            pltpu.VMEM((species // groups, 2 * LANES, nz), BF16),
            pltpu.VMEM((groups, x_cells, y_cells, LANES), F32),
            pltpu.VMEM((CORES * NX_CHIPS, x_cells, half_y, LANES), F32),
            *reduce_buffers(nz),
            *reduce_buffers(x_total),
            dma((5,)),
            dma((5,)),
            dma((5,)),
            dma((5,)),
            dma((species,)),
            dma((groups,)),
            dma,
            dma,
        ],
        compiler_params=pltpu.CompilerParams(
            collective_id=0, has_side_effects=True, vmem_limit_bytes=VMEM_LIMIT
        ),
        name="basis_core_gram",
    )(state_field, start_basis.T)

    column_count = y_cells * lax.axis_size("gy") * columns
    core_tensor, zt, x_triangle = pl.pallas_call(
        functools.partial(finish_kernel, column_count),
        out_shape=(
            jax.ShapeDtypeStruct((x_cells, y_cells, columns), F32),
            jax.ShapeDtypeStruct((rank, nz), F32),
            jax.ShapeDtypeStruct((x_total, x_total), F32),
        ),
        in_specs=[anywhere, vmem, vmem],
        out_specs=(anywhere, vmem, vmem),
        scratch_shapes=[pltpu.VMEM((x_total, x_total), F32), dma],
        compiler_params=pltpu.CompilerParams(vmem_limit_bytes=VMEM_LIMIT),
        name="x_factor",
    )(core_tensor, zt, gram_x)
    return core_tensor, zt.T, x_triangle


def solution(mesh):
    return jax.shard_map(
        local,
        mesh=mesh,
        in_specs=(P("gx", "gy", None, None), P()),
        out_specs=(P("gx", "gy", None), P(), P()),
        check_vma=False,
    )
```

```python
import functools
import math

import jax
import jax.numpy as jnp
from jax import lax
from jax.experimental import pallas as pl
from jax.experimental.pallas import tpu as pltpu
from jax.sharding import PartitionSpec as P

ITERS = 3
LANES = 128
SUBLANES = 8
MESH = pl.DeviceIdType.MESH
F32 = jnp.float32
BF16 = jnp.bfloat16
VMEM_LIMIT = 48 * 2**20

NX_CHIPS = 4
NY_CHIPS = 4
NZ_CHIPS = 8
CORES = 2
PLANE = NX_CHIPS * NY_CHIPS


def split3(value):
    high = value.astype(BF16)
    rest = value - high.astype(F32)
    middle = rest.astype(BF16)
    low = (rest - middle.astype(F32)).astype(BF16)
    return high, middle, low


def split2(value):
    high = value.astype(BF16)
    return high, (value - high.astype(F32)).astype(BF16)


def contract(left, right, left_dim, right_dim, precision=None):
    return lax.dot_general(
        left,
        right,
        (((left_dim,), (right_dim,)), ((), ())),
        precision=precision,
        preferred_element_type=F32,
    )


def lane_spread(block, lane):
    picks = jnp.full((SUBLANES, LANES), lane, jnp.int32)
    return jnp.take_along_axis(block, picks, axis=1, mode="promise_in_bounds")


def row_spread(block, row):
    return jnp.broadcast_to(block[row : row + 1, :], block.shape)


def eliminate(rows, tile, lane0):
    groups = len(rows)
    tiles = len(rows[0])
    rows = [list(group) for group in rows]
    sublane = lax.broadcasted_iota(jnp.int32, (SUBLANES, LANES), 0)
    steps = range(SUBLANES)
    for p in range(groups):
        below = range(p + 1, groups)
        columns = [
            {q: lane_spread(rows[q][tile], lane0 + SUBLANES * p + j) for q in range(p, groups)}
            for j in steps
        ]
        corner = {(j, l): row_spread(columns[l][p], j) for j in steps for l in range(j, SUBLANES)}
        lines = [[row_spread(rows[p][t], j) for j in steps] for t in range(tiles)]
        done = list(rows[p])
        for j in steps:
            inverse = 1.0 / corner[j, j]
            scale = lax.rsqrt(corner[j, j])
            for l in range(j + 1, SUBLANES):
                share = corner[j, l] * inverse
                for n in range(l, SUBLANES):
                    corner[l, n] = corner[l, n] - share * corner[j, n]
                for t in range(tiles):
                    lines[t][l] = lines[t][l] - share * lines[t][j]
            for q in below:
                factor = columns[j][q] * inverse
                for later in range(j + 1, SUBLANES):
                    columns[later][q] = columns[later][q] - factor * corner[j, later]
                for t in range(tiles):
                    rows[q][t] = rows[q][t] - factor * lines[t][j]
            for t in range(tiles):
                done[t] = jnp.where(sublane == j, lines[t][j] * scale, done[t])
        rows[p] = done
    return rows


def to_blocks(matrix):
    rows, columns = matrix.shape
    return [
        [
            matrix[r : r + SUBLANES, c : c + LANES]
            for c in range(0, columns, LANES)
        ]
        for r in range(0, rows, SUBLANES)
    ]


def from_blocks(blocks):
    return jnp.concatenate([jnp.concatenate(group, axis=1) for group in blocks], axis=0)


HIGHEST = lax.Precision.HIGHEST


def normalise(measured, image, transform):
    rank = measured.shape[0]
    inner_gram = contract(measured, measured, 1, 1, HIGHEST)
    padded = jnp.concatenate(
        [inner_gram, transform, jnp.zeros((rank, LANES - 2 * rank), F32)], axis=1
    )
    blocks = [[c[0]] + w for c, w in zip(to_blocks(padded), to_blocks(image))]
    blocks = eliminate(blocks, 0, 0)
    image = from_blocks([group[1:] for group in blocks])
    return image, from_blocks([group[:1] for group in blocks])[:, rank : 2 * rank]


def position():
    gx = lax.axis_index("gx")
    gy = lax.axis_index("gy")
    return gx // CORES, gx % CORES, gy % NY_CHIPS, gy // NY_CHIPS


def device(x, core, y, z):
    return (x * CORES + core, z * NY_CHIPS + y)


def far_first(steps):
    def hops(step):
        return sum(min(d, n - d) for d, n in zip(step, (NX_CHIPS, NY_CHIPS)))

    return sorted(steps, key=hops, reverse=True)


PLANE_STEPS = far_first(
    [(i, j) for i in range(NX_CHIPS) for j in range(NY_CHIPS) if i or j]
)
Z_STEPS = sorted(range(1, NZ_CHIPS), key=lambda d: -min(d, NZ_CHIPS - d))


def remote(source, target, send_sem, recv_sem, where):
    return pltpu.make_async_remote_copy(
        src_ref=source,
        dst_ref=target,
        send_sem=send_sem,
        recv_sem=recv_sem,
        device_id=where,
        device_id_type=MESH,
    )


def all_reduce(partial, full, from_core, mine, plane_in, z_out, z_in, send, recv):
    x, core, y, z = position()
    half = partial.shape[0] // CORES
    strip = half // PLANE
    place = x * NY_CHIPS + y
    own_half = pl.multiple_of(core * half, half)
    other_half = pl.multiple_of((1 - core) * half, half)
    other_core = device(x, 1 - core, y, z)

    swap = remote(
        partial.at[pl.ds(other_half, half)], from_core, send.at[0], recv.at[0], other_core
    )
    swap.start()
    swap.wait()
    summed = partial[pl.ds(own_half, half), :] + from_core[...]
    mine[...] = summed.reshape(mine.shape)

    for i, j in PLANE_STEPS:
        to_x, to_y = (x + i) % NX_CHIPS, (y + j) % NY_CHIPS
        remote(
            mine.at[to_x * NY_CHIPS + to_y],
            plane_in.at[place],
            send.at[1],
            recv.at[1],
            device(to_x, core, to_y, z),
        ).start()
    plane_in[place] = mine[place]
    others = pl.ds(0, PLANE - 1)
    landed = remote(mine.at[others], plane_in.at[others], send.at[1], recv.at[1], other_core)
    landed.wait()
    total = plane_in[0]
    for k in range(1, PLANE):
        total = total + plane_in[k]

    z_out[...] = total
    z_in[z] = total
    for d in Z_STEPS:
        to_z = (z + d) % NZ_CHIPS
        remote(
            z_out, z_in.at[z], send.at[2], recv.at[2], device(x, core, y, to_z)
        ).start()
    others = pl.ds(0, NZ_CHIPS - 1)
    landed = remote(z_in.at[others], z_in.at[others], send.at[2], recv.at[2], other_core)
    landed.wait()
    total = z_in[0]
    for k in range(1, NZ_CHIPS):
        total = total + z_in[k]

    own_strip = pl.ds(pl.multiple_of(own_half + place * strip, strip), strip)
    full[own_strip, :] = total
    for i, j in PLANE_STEPS:
        to_x, to_y = (x + i) % NX_CHIPS, (y + j) % NY_CHIPS
        remote(
            full.at[own_strip],
            full.at[own_strip],
            send.at[3],
            recv.at[3],
            device(to_x, core, to_y, z),
        ).start()
    others = pl.ds(0, (PLANE - 1) * strip)
    landed = remote(full.at[others], full.at[others], send.at[3], recv.at[3], other_core)
    landed.wait()

    rows = pl.ds(own_half, half)
    swap = remote(full.at[rows], full.at[rows], send.at[4], recv.at[4], other_core)
    swap.start()
    swap.wait()


def main_kernel(
    field,
    basis,
    core_out,
    zt_out,
    gram_x_out,
    staged,
    acc_same,
    acc_cross,
    partial,
    gram_z,
    gram_x,
    weights,
    weights_low,
    image_parts,
    core_parts,
    regrouped,
    normalised,
    basis_in,
    *scratch,
):
    reduce_z, reduce_x = scratch[0:5], scratch[5:10]
    send_z, recv_z, send_x, recv_x, load_sem, basis_sem, core_sem, cell_send, cell_recv = (
        scratch[10:]
    )
    x, core, y, z = position()
    gx = x * CORES + core
    species = staged.shape[0]
    x_cells, y_cells, nz = staged.shape[1:]
    cells = x_cells * y_cells
    rank = basis.shape[0]
    groups = species * rank // LANES
    per_group = species // groups

    for s in range(species):
        pltpu.make_async_copy(field.at[:, :, s, :], staged.at[s], load_sem.at[s]).start()

    pltpu.make_async_copy(basis, basis_in, basis_sem).start()

    barrier = pltpu.get_barrier_semaphore()
    partners = [device(x, 1 - core, y, z)]
    for i, j in PLANE_STEPS:
        partners.append(device((x + i) % NX_CHIPS, core, (y + j) % NY_CHIPS, z))
    for d in Z_STEPS:
        partners.append(device(x, core, y, (z + d) % NZ_CHIPS))
    for i in range(1, NX_CHIPS):
        partners.append(device((x + i) % NX_CHIPS, 1 - core, y, z))
    for partner in partners:
        pl.semaphore_signal(barrier, inc=1, device_id=partner, device_id_type=MESH)

    acc_same[...] = jnp.zeros_like(acc_same)
    acc_cross[...] = jnp.zeros_like(acc_cross)

    batch = 4

    def gram_step(i, carry):
        for s in range(batch):
            pltpu.make_async_copy(
                field.at[:, :, 0, :], staged.at[0], load_sem.at[i * batch + s]
            ).wait()
        slab = staged[pl.ds(i * batch, batch)].reshape(batch * cells, nz)
        high, middle = split2(slab)
        acc_same[...] += contract(high, high, 0, 0) + contract(middle, middle, 0, 0)
        acc_cross[...] += contract(high, middle, 0, 0)
        return carry

    lax.fori_loop(0, species // batch, gram_step, 0)
    cross = acc_cross[...]
    partial[...] = acc_same[...] + (cross + cross.T)

    pl.semaphore_wait(barrier, len(partners))
    all_reduce(partial, gram_z, *reduce_z, send_z, recv_z)

    pltpu.make_async_copy(basis, basis_in, basis_sem).wait()
    identity = (
        lax.broadcasted_iota(jnp.int32, (rank, rank), 0)
        == lax.broadcasted_iota(jnp.int32, (rank, rank), 1)
    ).astype(F32)

    def orth_pass(i, image):
        return normalise(image, image, identity)[0]

    vectors = contract(basis_in[...], gram_z[...], 1, 0, HIGHEST)
    vectors = lax.fori_loop(0, 2, orth_pass, vectors)
    for iteration in range(1, ITERS - 1):
        vectors = contract(vectors, gram_z[...], 1, 0, HIGHEST)
        vectors = normalise(vectors, vectors, identity)[0]
        if iteration < ITERS - 2:
            vectors = normalise(vectors, vectors, identity)[0]
    image = contract(vectors, gram_z[...], 1, 0, HIGHEST)

    b_high, b_middle, b_low = split3(image)
    weights[...] = jnp.zeros_like(weights)
    weights_low[...] = jnp.zeros_like(weights_low)
    for k in range(per_group):
        own = slice(k * rank, (k + 1) * rank)
        weights[k, own, :] = b_high
        weights[k, LANES + k * rank : LANES + (k + 1) * rank, :] = b_middle
        weights_low[k, own, :] = b_low

    half_y = y_cells // CORES
    parity = x % 2
    for order in range(groups):
        far = order < groups // 2
        to_core = order % CORES if far else (1 - core if order == groups // 2 else core)
        g = ((1 - parity) if far else parity) * CORES + to_core
        total = jnp.zeros((cells, 2 * LANES), F32)
        rest = jnp.zeros((cells, LANES), F32)
        for k in range(per_group):
            high, middle, low = split3(staged[g * per_group + k].reshape(cells, nz))
            total += contract(high, weights[k], 1, 1) + contract(middle, weights[k], 1, 1)
            rest += contract(low, weights[k, :LANES], 1, 1) + contract(high, weights_low[k], 1, 1)
        image_parts[g] = (total[:, :LANES] + (total[:, LANES:] + rest)).reshape(
            x_cells, y_cells, LANES
        )
        if far:
            targets = [(x + 1) % NX_CHIPS, (x + 3) % NX_CHIPS]
        elif order == groups // 2:
            targets = [(x + 2) % NX_CHIPS, x]
        else:
            targets = [(x + 2) % NX_CHIPS]
        for to_x in targets:
            there = pl.multiple_of(to_x // 2 * half_y, half_y)
            remote(
                image_parts.at[g, :, pl.ds(there, half_y), :],
                regrouped.at[gx],
                cell_send,
                cell_recv.at[gx],
                device(to_x, to_core, y, z),
            ).start()
        if order == groups - 1:
            here = pl.multiple_of(x // 2 * half_y, half_y)
            regrouped[gx] = image_parts[g, :, pl.ds(here, half_y), :]

    def last_pass(i, carry):
        measured, image, transform = carry
        image, transform = normalise(measured, image, transform)
        return image, image, transform

    _, basis_t, transform = lax.fori_loop(0, 3, last_pass, (vectors, image, identity))
    zt_out[...] = basis_t

    z_high, z_middle = split2(basis_t)
    for k in range(per_group):
        weights[k, k * rank : (k + 1) * rank, :] = z_high
        weights[k, LANES + k * rank : LANES + (k + 1) * rank, :] = z_middle
    for g in range(groups):
        total = jnp.zeros((cells, 2 * LANES), F32)
        for k in range(per_group):
            high, middle = split2(staged[g * per_group + k].reshape(cells, nz))
            total += contract(high, weights[k], 1, 1) + contract(middle, weights[k], 1, 1)
        core_parts[g] = (total[:, :LANES] + total[:, LANES:]).reshape(
            x_cells, y_cells, LANES
        )
        pltpu.make_async_copy(
            core_parts.at[g], core_out.at[:, :, pl.ds(g * LANES, LANES)], core_sem.at[g]
        ).start()

    wide = jnp.concatenate([transform] * per_group, axis=1)
    wide = jnp.concatenate([wide] * per_group, axis=0)
    row = lax.broadcasted_iota(jnp.int32, wide.shape, 0) // rank
    lane = lax.broadcasted_iota(jnp.int32, wide.shape, 1) // rank
    wide = jnp.where(row == lane, wide, 0.0)

    chunk_rows = x_cells * half_y
    for i, j in ((0, 0), (0, 1), (1, 0), (3, 0), (1, 1), (3, 1), (2, 1), (2, 0)):
        source = (x + i) % NX_CHIPS * CORES + (core + j) % CORES
        if i or j:
            remote(
                regrouped.at[source],
                regrouped.at[source],
                cell_send,
                cell_recv.at[source],
                partners[0],
            ).wait_recv()
        rows = pl.ds(pl.multiple_of(source * chunk_rows, chunk_rows), chunk_rows)
        normalised[rows, :] = contract(
            regrouped[source].reshape(chunk_rows, LANES), wide, 1, 1, HIGHEST
        )
    others = pl.ds(0, CORES * NX_CHIPS - 1)
    remote(
        regrouped.at[others], regrouped.at[others], cell_send, cell_recv.at[0], partners[0]
    ).wait_send()

    total_rows = regrouped.shape[0] * x_cells
    table = normalised
    same = jnp.zeros((total_rows, total_rows), F32)
    cross = jnp.zeros((total_rows, total_rows), F32)
    for pair in range(half_y // 2):
        both = jnp.concatenate(
            [table[pl.ds(2 * pair + i, total_rows, stride=half_y), :] for i in range(2)],
            axis=1,
        )
        high, middle, low = split3(both)
        same += contract(high, high, 1, 1) + contract(middle, middle, 1, 1)
        cross += contract(high, middle, 1, 1) + contract(high, low, 1, 1)
    partial[...] = same + (cross + cross.T)
    all_reduce(partial, gram_x, *reduce_x, send_x, recv_x)
    gram_x_out[...] = gram_x[...]
    for g in range(groups):
        pltpu.make_async_copy(
            core_parts.at[0], core_out.at[:, :, pl.ds(0, LANES)], core_sem.at[g]
        ).wait()


def finish_kernel(column_count, core_in, zt, gram_x, core_out, z_out, tri_out, upper, sem):
    copy = pltpu.make_async_copy(core_in, core_out, sem)
    copy.start()
    z_out[...] = zt[...]
    size = gram_x.shape[0]
    block = 64
    scale = 1.0 / math.sqrt(column_count)
    for r in range(0, size, block):
        first = r // LANES * LANES
        here = gram_x[r : r + block, first:]
        if r:
            here = here - contract(
                upper[0:r, r : r + block], upper[0:r, first:], 0, 0, HIGHEST
            )
        done = from_blocks(eliminate(to_blocks(here), 0, r - first))
        row = lax.broadcasted_iota(jnp.int32, done.shape, 0) + r
        column = lax.broadcasted_iota(jnp.int32, done.shape, 1) + first
        done = jnp.where(column >= row, done, 0.0)
        upper[r : r + block, first:] = done
        tri_out[r : r + block, first:] = done * scale
        if first:
            tri_out[r : r + block, :first] = jnp.zeros((block, first), F32)
    copy.wait()


def local(state_field, start_basis):
    x_cells, y_cells, species, nz = state_field.shape
    rank = start_basis.shape[1]
    columns = species * rank
    x_total = x_cells * lax.axis_size("gx")
    groups = columns // LANES
    half_y = y_cells // CORES
    vmem = pl.BlockSpec(memory_space=pltpu.VMEM)
    anywhere = pl.BlockSpec(memory_space=pl.ANY)

    def reduce_buffers(size):
        half = size // CORES
        strip = half // PLANE
        return [
            pltpu.VMEM((half, size), F32),
            pltpu.VMEM((PLANE, strip, size), F32),
            pltpu.VMEM((PLANE, strip, size), F32),
            pltpu.VMEM((strip, size), F32),
            pltpu.VMEM((NZ_CHIPS, strip, size), F32),
        ]

    dma = pltpu.SemaphoreType.DMA
    core_tensor, zt, gram_x = pl.pallas_call(
        main_kernel,
        out_shape=(
            jax.ShapeDtypeStruct((x_cells, y_cells, columns), F32),
            jax.ShapeDtypeStruct((rank, nz), F32),
            jax.ShapeDtypeStruct((x_total, x_total), F32),
        ),
        in_specs=[anywhere, pl.BlockSpec(memory_space=pltpu.HBM)],
        out_specs=(anywhere, vmem, vmem),
        scratch_shapes=[
            pltpu.VMEM((species, x_cells, y_cells, nz), F32),
            pltpu.VMEM((nz, nz), F32),
            pltpu.VMEM((nz, nz), F32),
            pltpu.VMEM((nz, nz), F32),
            pltpu.VMEM((nz, nz), F32),
            pltpu.VMEM((x_total, x_total), F32),
            pltpu.VMEM((species // groups, 2 * LANES, nz), BF16),
            pltpu.VMEM((species // groups, LANES, nz), BF16),
            pltpu.VMEM((groups, x_cells, y_cells, LANES), F32),
            pltpu.VMEM((groups, x_cells, y_cells, LANES), F32),
            pltpu.VMEM((CORES * NX_CHIPS, x_cells, half_y, LANES), F32),
            pltpu.VMEM((x_total * half_y, LANES), F32),
            pltpu.VMEM((rank, nz), F32),
            *reduce_buffers(nz),
            *reduce_buffers(x_total),
            dma((5,)),
            dma((5,)),
            dma((5,)),
            dma((5,)),
            dma((species,)),
            dma,
            dma((groups,)),
            dma,
            dma((CORES * NX_CHIPS,)),
        ],
        compiler_params=pltpu.CompilerParams(
            collective_id=0, has_side_effects=True, vmem_limit_bytes=VMEM_LIMIT
        ),
        name="basis_core_gram",
    )(state_field, start_basis.T)

    column_count = y_cells * lax.axis_size("gy") * columns
    core_tensor, zt, x_triangle = pl.pallas_call(
        functools.partial(finish_kernel, column_count),
        out_shape=(
            jax.ShapeDtypeStruct((x_cells, y_cells, columns), F32),
            jax.ShapeDtypeStruct((rank, nz), F32),
            jax.ShapeDtypeStruct((x_total, x_total), F32),
        ),
        in_specs=[anywhere, vmem, vmem],
        out_specs=(anywhere, vmem, vmem),
        scratch_shapes=[pltpu.VMEM((x_total, x_total), F32), dma],
        compiler_params=pltpu.CompilerParams(vmem_limit_bytes=VMEM_LIMIT),
        name="x_factor",
    )(core_tensor, zt, gram_x)
    return core_tensor, zt.T, x_triangle


def solution(mesh):
    return jax.shard_map(
        local,
        mesh=mesh,
        in_specs=(P("gx", "gy", None, None), P()),
        out_specs=(P("gx", "gy", None), P(), P()),
        check_vma=False,
    )
```

```python
import functools
import math

import jax
import jax.numpy as jnp
from jax import lax
from jax.experimental import pallas as pl
from jax.experimental.pallas import tpu as pltpu
from jax.sharding import PartitionSpec as P

ITERS = 3
LANES = 128
SUBLANES = 8
MESH = pl.DeviceIdType.MESH
F32 = jnp.float32
BF16 = jnp.bfloat16
VMEM_LIMIT = 48 * 2**20

NX_CHIPS = 4
NY_CHIPS = 4
NZ_CHIPS = 8
CORES = 2
PLANE = NX_CHIPS * NY_CHIPS


def split3(value):
    high = value.astype(BF16)
    rest = value - high.astype(F32)
    middle = rest.astype(BF16)
    low = (rest - middle.astype(F32)).astype(BF16)
    return high, middle, low


def split2(value):
    high = value.astype(BF16)
    return high, (value - high.astype(F32)).astype(BF16)


def contract(left, right, left_dim, right_dim, precision=None):
    return lax.dot_general(
        left,
        right,
        (((left_dim,), (right_dim,)), ((), ())),
        precision=precision,
        preferred_element_type=F32,
    )


def lane_spread(block, lane):
    picks = jnp.full((SUBLANES, LANES), lane, jnp.int32)
    return jnp.take_along_axis(block, picks, axis=1, mode="promise_in_bounds")


def row_spread(block, row):
    return jnp.broadcast_to(block[row : row + 1, :], block.shape)


def eliminate(rows, tile, lane0):
    groups = len(rows)
    tiles = len(rows[0])
    rows = [list(group) for group in rows]
    sublane = lax.broadcasted_iota(jnp.int32, (SUBLANES, LANES), 0)
    steps = range(SUBLANES)
    for p in range(groups):
        below = range(p + 1, groups)
        columns = [
            {q: lane_spread(rows[q][tile], lane0 + SUBLANES * p + j) for q in range(p, groups)}
            for j in steps
        ]
        corner = {(j, l): row_spread(columns[l][p], j) for j in steps for l in range(j, SUBLANES)}
        lines = [[row_spread(rows[p][t], j) for j in steps] for t in range(tiles)]
        done = list(rows[p])
        for j in steps:
            inverse = 1.0 / corner[j, j]
            scale = lax.rsqrt(corner[j, j])
            for l in range(j + 1, SUBLANES):
                share = corner[j, l] * inverse
                for n in range(l, SUBLANES):
                    corner[l, n] = corner[l, n] - share * corner[j, n]
                for t in range(tiles):
                    lines[t][l] = lines[t][l] - share * lines[t][j]
            for q in below:
                factor = columns[j][q] * inverse
                for later in range(j + 1, SUBLANES):
                    columns[later][q] = columns[later][q] - factor * corner[j, later]
                for t in range(tiles):
                    rows[q][t] = rows[q][t] - factor * lines[t][j]
            for t in range(tiles):
                done[t] = jnp.where(sublane == j, lines[t][j] * scale, done[t])
        rows[p] = done
    return rows


def to_blocks(matrix):
    rows, columns = matrix.shape
    return [
        [
            matrix[r : r + SUBLANES, c : c + LANES]
            for c in range(0, columns, LANES)
        ]
        for r in range(0, rows, SUBLANES)
    ]


def from_blocks(blocks):
    return jnp.concatenate([jnp.concatenate(group, axis=1) for group in blocks], axis=0)


HIGHEST = lax.Precision.HIGHEST


def normalise(measured, image, transform):
    rank = measured.shape[0]
    inner_gram = contract(measured, measured, 1, 1, HIGHEST)
    padded = jnp.concatenate(
        [inner_gram, transform, jnp.zeros((rank, LANES - 2 * rank), F32)], axis=1
    )
    blocks = [[c[0]] + w for c, w in zip(to_blocks(padded), to_blocks(image))]
    blocks = eliminate(blocks, 0, 0)
    image = from_blocks([group[1:] for group in blocks])
    return image, from_blocks([group[:1] for group in blocks])[:, rank : 2 * rank]


def position():
    gx = lax.axis_index("gx")
    gy = lax.axis_index("gy")
    return gx // CORES, gx % CORES, gy % NY_CHIPS, gy // NY_CHIPS


def device(x, core, y, z):
    return (x * CORES + core, z * NY_CHIPS + y)


def far_first(steps):
    def hops(step):
        return sum(min(d, n - d) for d, n in zip(step, (NX_CHIPS, NY_CHIPS)))

    return sorted(steps, key=hops, reverse=True)


PLANE_STEPS = far_first(
    [(i, j) for i in range(NX_CHIPS) for j in range(NY_CHIPS) if i or j]
)
Z_STEPS = sorted(range(1, NZ_CHIPS), key=lambda d: -min(d, NZ_CHIPS - d))


def remote(source, target, send_sem, recv_sem, where):
    return pltpu.make_async_remote_copy(
        src_ref=source,
        dst_ref=target,
        send_sem=send_sem,
        recv_sem=recv_sem,
        device_id=where,
        device_id_type=MESH,
    )


def all_reduce(partial, full, from_core, mine, plane_in, z_out, z_in, send, recv):
    x, core, y, z = position()
    half = partial.shape[0] // CORES
    strip = half // PLANE
    place = x * NY_CHIPS + y
    own_half = pl.multiple_of(core * half, half)
    other_half = pl.multiple_of((1 - core) * half, half)
    other_core = device(x, 1 - core, y, z)

    swap = remote(
        partial.at[pl.ds(other_half, half)], from_core, send.at[0], recv.at[0], other_core
    )
    swap.start()
    swap.wait()
    summed = partial[pl.ds(own_half, half), :] + from_core[...]
    mine[...] = summed.reshape(mine.shape)

    for i, j in PLANE_STEPS:
        to_x, to_y = (x + i) % NX_CHIPS, (y + j) % NY_CHIPS
        remote(
            mine.at[to_x * NY_CHIPS + to_y],
            plane_in.at[place],
            send.at[1],
            recv.at[1],
            device(to_x, core, to_y, z),
        ).start()
    plane_in[place] = mine[place]
    others = pl.ds(0, PLANE - 1)
    landed = remote(mine.at[others], plane_in.at[others], send.at[1], recv.at[1], other_core)
    landed.wait()
    total = plane_in[0]
    for k in range(1, PLANE):
        total = total + plane_in[k]

    z_out[...] = total
    z_in[z] = total
    for d in Z_STEPS:
        to_z = (z + d) % NZ_CHIPS
        remote(
            z_out, z_in.at[z], send.at[2], recv.at[2], device(x, core, y, to_z)
        ).start()
    others = pl.ds(0, NZ_CHIPS - 1)
    landed = remote(z_in.at[others], z_in.at[others], send.at[2], recv.at[2], other_core)
    landed.wait()
    total = z_in[0]
    for k in range(1, NZ_CHIPS):
        total = total + z_in[k]

    own_strip = pl.ds(pl.multiple_of(own_half + place * strip, strip), strip)
    full[own_strip, :] = total
    for i, j in PLANE_STEPS:
        to_x, to_y = (x + i) % NX_CHIPS, (y + j) % NY_CHIPS
        remote(
            full.at[own_strip],
            full.at[own_strip],
            send.at[3],
            recv.at[3],
            device(to_x, core, to_y, z),
        ).start()
    others = pl.ds(0, (PLANE - 1) * strip)
    landed = remote(full.at[others], full.at[others], send.at[3], recv.at[3], other_core)
    landed.wait()

    rows = pl.ds(own_half, half)
    swap = remote(full.at[rows], full.at[rows], send.at[4], recv.at[4], other_core)
    swap.start()
    swap.wait()


def main_kernel(
    field,
    basis,
    core_out,
    zt_out,
    gram_x_out,
    staged,
    acc_same,
    acc_cross,
    partial,
    gram_z,
    gram_x,
    weights,
    weights_low,
    image_parts,
    core_parts,
    regrouped,
    normalised,
    basis_in,
    *scratch,
):
    reduce_z, reduce_x = scratch[0:5], scratch[5:10]
    send_z, recv_z, send_x, recv_x, load_sem, basis_sem, core_sem, cell_send, cell_recv = (
        scratch[10:]
    )
    x, core, y, z = position()
    gx = x * CORES + core
    species = staged.shape[0]
    x_cells, y_cells, nz = staged.shape[1:]
    cells = x_cells * y_cells
    rank = basis.shape[0]
    groups = species * rank // LANES
    per_group = species // groups

    for s in range(species):
        pltpu.make_async_copy(field.at[:, :, s, :], staged.at[s], load_sem.at[s]).start()

    pltpu.make_async_copy(basis, basis_in, basis_sem).start()

    barrier = pltpu.get_barrier_semaphore()
    partners = [device(x, 1 - core, y, z)]
    for i, j in PLANE_STEPS:
        partners.append(device((x + i) % NX_CHIPS, core, (y + j) % NY_CHIPS, z))
    for d in Z_STEPS:
        partners.append(device(x, core, y, (z + d) % NZ_CHIPS))
    for i in range(1, NX_CHIPS):
        partners.append(device((x + i) % NX_CHIPS, 1 - core, y, z))
    for partner in partners:
        pl.semaphore_signal(barrier, inc=1, device_id=partner, device_id_type=MESH)

    weights[...] = jnp.zeros_like(weights)
    weights_low[...] = jnp.zeros_like(weights_low)
    acc_same[...] = jnp.zeros_like(acc_same)
    acc_cross[...] = jnp.zeros_like(acc_cross)

    batch = 4

    def gram_step(i, carry):
        for s in range(batch):
            pltpu.make_async_copy(
                field.at[:, :, 0, :], staged.at[0], load_sem.at[i * batch + s]
            ).wait()
        slab = staged[pl.ds(i * batch, batch)].reshape(batch * cells, nz)
        high, middle = split2(slab)
        acc_same[...] += contract(high, high, 0, 0) + contract(middle, middle, 0, 0)
        acc_cross[...] += contract(high, middle, 0, 0)
        return carry

    lax.fori_loop(0, species // batch, gram_step, 0)
    cross = acc_cross[...]
    partial[...] = acc_same[...] + (cross + cross.T)

    pl.semaphore_wait(barrier, len(partners))
    all_reduce(partial, gram_z, *reduce_z, send_z, recv_z)

    pltpu.make_async_copy(basis, basis_in, basis_sem).wait()
    identity = (
        lax.broadcasted_iota(jnp.int32, (rank, rank), 0)
        == lax.broadcasted_iota(jnp.int32, (rank, rank), 1)
    ).astype(F32)

    def orth_pass(i, image):
        return normalise(image, image, identity)[0]

    vectors = contract(basis_in[...], gram_z[...], 1, 0, HIGHEST)
    vectors = lax.fori_loop(0, 2, orth_pass, vectors)
    for iteration in range(1, ITERS - 1):
        vectors = contract(vectors, gram_z[...], 1, 0, HIGHEST)
        vectors = normalise(vectors, vectors, identity)[0]
        if iteration < ITERS - 2:
            vectors = normalise(vectors, vectors, identity)[0]
    image = contract(vectors, gram_z[...], 1, 0, HIGHEST)

    b_high, b_middle, b_low = split3(image)
    for k in range(per_group):
        own = slice(k * rank, (k + 1) * rank)
        weights[k, own, :] = b_high
        weights[k, LANES + k * rank : LANES + (k + 1) * rank, :] = b_middle
        weights_low[k, own, :] = b_low

    half_y = y_cells // CORES
    parity = x % 2
    for order in range(groups):
        far = order < groups // 2
        to_core = order % CORES if far else (1 - core if order == groups // 2 else core)
        g = ((1 - parity) if far else parity) * CORES + to_core
        total = jnp.zeros((cells, 2 * LANES), F32)
        rest = jnp.zeros((cells, LANES), F32)
        for k in range(per_group):
            high, middle, low = split3(staged[g * per_group + k].reshape(cells, nz))
            total += contract(high, weights[k], 1, 1) + contract(middle, weights[k], 1, 1)
            rest += contract(low, weights[k, :LANES], 1, 1) + contract(high, weights_low[k], 1, 1)
        image_parts[g] = (total[:, :LANES] + (total[:, LANES:] + rest)).reshape(
            x_cells, y_cells, LANES
        )
        if far:
            targets = [(x + 1) % NX_CHIPS, (x + 3) % NX_CHIPS]
        elif order == groups // 2:
            targets = [(x + 2) % NX_CHIPS, x]
        else:
            targets = [(x + 2) % NX_CHIPS]
        for to_x in targets:
            there = pl.multiple_of(to_x // 2 * half_y, half_y)
            remote(
                image_parts.at[g, :, pl.ds(there, half_y), :],
                regrouped.at[gx],
                cell_send,
                cell_recv.at[gx],
                device(to_x, to_core, y, z),
            ).start()
        if order == groups - 1:
            here = pl.multiple_of(x // 2 * half_y, half_y)
            regrouped[gx] = image_parts[g, :, pl.ds(here, half_y), :]

    def last_pass(i, carry):
        measured, image, transform = carry
        image, transform = normalise(measured, image, transform)
        return image, image, transform

    _, basis_t, transform = lax.fori_loop(0, 3, last_pass, (vectors, image, identity))
    zt_out[...] = basis_t

    z_high, z_middle = split2(basis_t)
    for k in range(per_group):
        weights[k, k * rank : (k + 1) * rank, :] = z_high
        weights[k, LANES + k * rank : LANES + (k + 1) * rank, :] = z_middle
    for g in range(groups):
        total = jnp.zeros((cells, 2 * LANES), F32)
        for k in range(per_group):
            high, middle = split2(staged[g * per_group + k].reshape(cells, nz))
            total += contract(high, weights[k], 1, 1) + contract(middle, weights[k], 1, 1)
        core_parts[g] = (total[:, :LANES] + total[:, LANES:]).reshape(
            x_cells, y_cells, LANES
        )
        pltpu.make_async_copy(
            core_parts.at[g], core_out.at[:, :, pl.ds(g * LANES, LANES)], core_sem.at[g]
        ).start()

    wide = jnp.concatenate([transform] * per_group, axis=1)
    wide = jnp.concatenate([wide] * per_group, axis=0)
    row = lax.broadcasted_iota(jnp.int32, wide.shape, 0) // rank
    lane = lax.broadcasted_iota(jnp.int32, wide.shape, 1) // rank
    wide = jnp.where(row == lane, wide, 0.0)

    chunk_rows = x_cells * half_y
    for i, j in ((0, 0), (0, 1), (1, 0), (3, 0), (1, 1), (3, 1), (2, 1), (2, 0)):
        source = (x + i) % NX_CHIPS * CORES + (core + j) % CORES
        if i or j:
            remote(
                regrouped.at[source],
                regrouped.at[source],
                cell_send,
                cell_recv.at[source],
                partners[0],
            ).wait_recv()
        rows = pl.ds(pl.multiple_of(source * chunk_rows, chunk_rows), chunk_rows)
        normalised[rows, :] = contract(
            regrouped[source].reshape(chunk_rows, LANES), wide, 1, 1, HIGHEST
        )
    others = pl.ds(0, CORES * NX_CHIPS - 1)
    remote(
        regrouped.at[others], regrouped.at[others], cell_send, cell_recv.at[0], partners[0]
    ).wait_send()

    total_rows = regrouped.shape[0] * x_cells
    table = normalised
    same = jnp.zeros((total_rows, total_rows), F32)
    cross = jnp.zeros((total_rows, total_rows), F32)
    for pair in range(half_y // 2):
        both = jnp.concatenate(
            [table[pl.ds(2 * pair + i, total_rows, stride=half_y), :] for i in range(2)],
            axis=1,
        )
        high, middle, low = split3(both)
        same += contract(high, high, 1, 1) + contract(middle, middle, 1, 1)
        cross += contract(high, middle, 1, 1) + contract(high, low, 1, 1)
    partial[...] = same + (cross + cross.T)
    all_reduce(partial, gram_x, *reduce_x, send_x, recv_x)
    gram_x_out[...] = gram_x[...]
    for g in range(groups):
        pltpu.make_async_copy(
            core_parts.at[0], core_out.at[:, :, pl.ds(0, LANES)], core_sem.at[g]
        ).wait()


def finish_kernel(column_count, core_in, zt, gram_x, core_out, z_out, tri_out, upper, sem):
    copy = pltpu.make_async_copy(core_in, core_out, sem)
    copy.start()
    z_out[...] = zt[...]
    size = gram_x.shape[0]
    block = 64
    scale = 1.0 / math.sqrt(column_count)
    for r in range(0, size, block):
        first = r // LANES * LANES
        here = gram_x[r : r + block, first:]
        if r:
            here = here - contract(
                upper[0:r, r : r + block], upper[0:r, first:], 0, 0, HIGHEST
            )
        done = from_blocks(eliminate(to_blocks(here), 0, r - first))
        row = lax.broadcasted_iota(jnp.int32, done.shape, 0) + r
        column = lax.broadcasted_iota(jnp.int32, done.shape, 1) + first
        done = jnp.where(column >= row, done, 0.0)
        upper[r : r + block, first:] = done
        tri_out[r : r + block, first:] = done * scale
        if first:
            tri_out[r : r + block, :first] = jnp.zeros((block, first), F32)
    copy.wait()


def local(state_field, start_basis):
    x_cells, y_cells, species, nz = state_field.shape
    rank = start_basis.shape[1]
    columns = species * rank
    x_total = x_cells * lax.axis_size("gx")
    groups = columns // LANES
    half_y = y_cells // CORES
    vmem = pl.BlockSpec(memory_space=pltpu.VMEM)
    anywhere = pl.BlockSpec(memory_space=pl.ANY)

    def reduce_buffers(size):
        half = size // CORES
        strip = half // PLANE
        return [
            pltpu.VMEM((half, size), F32),
            pltpu.VMEM((PLANE, strip, size), F32),
            pltpu.VMEM((PLANE, strip, size), F32),
            pltpu.VMEM((strip, size), F32),
            pltpu.VMEM((NZ_CHIPS, strip, size), F32),
        ]

    dma = pltpu.SemaphoreType.DMA
    core_tensor, zt, gram_x = pl.pallas_call(
        main_kernel,
        out_shape=(
            jax.ShapeDtypeStruct((x_cells, y_cells, columns), F32),
            jax.ShapeDtypeStruct((rank, nz), F32),
            jax.ShapeDtypeStruct((x_total, x_total), F32),
        ),
        in_specs=[anywhere, pl.BlockSpec(memory_space=pltpu.HBM)],
        out_specs=(anywhere, vmem, vmem),
        scratch_shapes=[
            pltpu.VMEM((species, x_cells, y_cells, nz), F32),
            pltpu.VMEM((nz, nz), F32),
            pltpu.VMEM((nz, nz), F32),
            pltpu.VMEM((nz, nz), F32),
            pltpu.VMEM((nz, nz), F32),
            pltpu.VMEM((x_total, x_total), F32),
            pltpu.VMEM((species // groups, 2 * LANES, nz), BF16),
            pltpu.VMEM((species // groups, LANES, nz), BF16),
            pltpu.VMEM((groups, x_cells, y_cells, LANES), F32),
            pltpu.VMEM((groups, x_cells, y_cells, LANES), F32),
            pltpu.VMEM((CORES * NX_CHIPS, x_cells, half_y, LANES), F32),
            pltpu.VMEM((x_total * half_y, LANES), F32),
            pltpu.VMEM((rank, nz), F32),
            *reduce_buffers(nz),
            *reduce_buffers(x_total),
            dma((5,)),
            dma((5,)),
            dma((5,)),
            dma((5,)),
            dma((species,)),
            dma,
            dma((groups,)),
            dma,
            dma((CORES * NX_CHIPS,)),
        ],
        compiler_params=pltpu.CompilerParams(
            collective_id=0, has_side_effects=True, vmem_limit_bytes=VMEM_LIMIT
        ),
        name="basis_core_gram",
    )(state_field, start_basis.T)

    column_count = y_cells * lax.axis_size("gy") * columns
    core_tensor, zt, x_triangle = pl.pallas_call(
        functools.partial(finish_kernel, column_count),
        out_shape=(
            jax.ShapeDtypeStruct((x_cells, y_cells, columns), F32),
            jax.ShapeDtypeStruct((rank, nz), F32),
            jax.ShapeDtypeStruct((x_total, x_total), F32),
        ),
        in_specs=[anywhere, vmem, vmem],
        out_specs=(anywhere, vmem, vmem),
        scratch_shapes=[pltpu.VMEM((x_total, x_total), F32), dma],
        compiler_params=pltpu.CompilerParams(vmem_limit_bytes=VMEM_LIMIT),
        name="x_factor",
    )(core_tensor, zt, gram_x)
    return core_tensor, zt.T, x_triangle


def solution(mesh):
    return jax.shard_map(
        local,
        mesh=mesh,
        in_specs=(P("gx", "gy", None, None), P()),
        out_specs=(P("gx", "gy", None), P(), P()),
        check_vma=False,
    )
```
